32 devices in a mesh: grp: 2 (over y), scan: 4 (over z), view: 2 (over x), pix: 2 (over core).
Axes of the slice: x: 2, y: 2, z: 4, core: 2. Of those that a mesh axis runs over, the one named last changes fastest.
Arguments:
- frames: bfloat16 [16, 128, 8192], P(('grp', 'view'), 'scan', 'pix'), parts along dimension 0, may hold values from -6 to 6
- tile_values: bfloat16 [16, 8, 128, 128], P(None, 'pix'), may hold values from -0.21875 to 0.21875
- tile_index: int32 [16, 8], P(None, 'pix'), may hold values from 0 to 63, as said below
- tile_mask: int32 [16, 8], P(None, 'pix'), may hold values 0 or 1
- angle_index: int32 [8], replicated, may hold values from 0 to 179
Outputs:
- slices: bfloat16 [4096, 32, 2048], P(('grp', 'scan'), ('view', 'pix')), parts along dimension 0
The draws below stay inside these ranges and needn't reach their ends.
There are 2 independent parts, one for each index of `grp`. The reference program is written for one: setup_inputs(seed, part) draws one part's arguments, and reference() takes and returns one part's arrays. A program takes and returns all parts, laid end to end along the dimension named above; an argument that names none is the same for every part. Nothing has to cross between parts.
Inputs may be any that keep to these rules, and one draw needn't show every extreme that they name: `tile_index`: entry k of each block's list names a detector tile of the pixel half k // 4, a number from (k // 4) * 32 to (k // 4 + 1) * 32 - 1; a list may name a tile twice.
All inputs are finite; a program needn't handle non-finite values. No bound on the sum of `tile_mask` on one device may be relied on, other than what follows from the above.
Results may differ from the reference program's by a relative error of at most 0.007.
Values may be sent and summed in bfloat16 or wider, within the bound.
No kernel may reach another device: no remote copies, remote signals or barrier semaphores. Data moves between devices by JAX's collectives and lax.ppermute only.
A program may use at most 512 MiB of HBM per device.

```python
import math
import jax
import jax.numpy as jnp
from jax import lax

Q = 2048
TILE = 128
NANG = 180
ROT = 8
NT_DEV = 32
KT_DEV = 4
COLS = 2048
NT = 64
PIXELS = 8192
KT = 8
QBLK = 16
PTS = 128
ROWS = 32


def draw_tile_index(key, part):
    key = jax.random.fold_in(key, 7)
    half_of = (jnp.arange(KT) // KT_DEV).astype(jnp.int32)
    listed = jax.random.randint(key, (QBLK, KT), 0, NT_DEV, dtype=jnp.int32) + half_of[None, :] * NT_DEV
    listed = listed.at[0, 0].set(0)
    listed = listed.at[QBLK - 1, KT - 1].set(NT - 1)
    return listed


def touch_ends(drawn, rng, low, high):
    longest = drawn.shape.index(max(drawn.shape))
    spots = []
    for shift in (0, 1):
        where = [jax.random.randint(jax.random.fold_in(rng, axis), (), 0, length) for axis, length in enumerate(drawn.shape)]
        where[longest] = (where[longest] + shift) % drawn.shape[longest]
        spots.append(tuple(where))
    return drawn.at[spots[0]].set(low).at[spots[1]].set(high)


def block_levels(stream_key, shape, cuts, low, high):
    loudness = 1.0
    for dim, blocks in cuts:
        draws = jax.random.uniform(jax.random.fold_in(jax.random.fold_in(stream_key, 6), dim), (blocks,), jnp.float32, low / len(cuts), high / len(cuts))
        loudness = loudness * jnp.repeat(jnp.exp(draws), shape[dim] // blocks).reshape((-1,) + (1,) * (len(shape) - 1 - dim))
    return loudness


def scatter_about(stream_key, dims, spread, reach, cuts=(), held_as=jnp.bfloat16):
    values = spread * jax.random.normal(stream_key, dims, jnp.float32)
    if cuts:
        values = values * block_levels(stream_key, dims, cuts, -0.22, 0.18)
    return jnp.clip(values, -reach, reach).astype(held_as)


def setup_inputs(seed: int = 0, part: int = 0) -> dict:
    splits = jax.random.split(jax.random.key(seed), 6)
    part_keys = jax.random.split(jax.random.fold_in(splits[5], part), 6)
    return {
        "frames": scatter_about(part_keys[0], (ROT, PTS, PIXELS), 1.0, 6.0, ((0, 2), (1, 4), (2, 2))),
        "tile_values": scatter_about(splits[1], (QBLK, KT, TILE, TILE), (KT * 96) ** -0.5, 0.21875, ((1, 2),)),
        "tile_index": draw_tile_index(jax.random.fold_in(splits[5], 71), part),
        "tile_mask": touch_ends((jax.random.randint(splits[3], (QBLK, KT), 0, 4) < 3).astype(jnp.int32), jax.random.fold_in(splits[3], 1), 0, 1),
        "angle_index": touch_ends(jax.random.randint(splits[4], (ROT,), 0, NANG), jax.random.fold_in(splits[4], 1), 0, NANG - 1).astype(jnp.int32),
    }


def ramp_matrix(points):
    offset = (jnp.arange(points)[:, None] - jnp.arange(points)[None, :]).astype(jnp.int32)
    is_odd = (offset % 2) == 1
    distance = offset.astype(jnp.float32)
    safe_offset = jnp.where(is_odd, distance, 1.0)
    kernel = jnp.where(is_odd, -1.0 / (math.pi * math.pi * safe_offset * safe_offset), 0.0)
    kernel = jnp.where(offset == 0, 0.25, kernel)
    return kernel.astype(jnp.bfloat16)


def reference(frames, tile_values, tile_index, tile_mask, angle_index):
    flat_frames = frames.reshape(ROT * PTS, NT, TILE)

    def one_block(element):
        block_values, block_index, block_mask = element
        pieces = jnp.take(flat_frames, block_index.astype(jnp.int32), axis=1)
        pieces = pieces * block_mask.astype(jnp.bfloat16)[None, :, None]
        return jnp.einsum("skp,kpq->sq", pieces.astype(jnp.float32), block_values.astype(jnp.float32))

    block_sums = lax.map(one_block, (tile_values, tile_index, tile_mask))
    patterns = block_sums.transpose(1, 0, 2).reshape(ROT, PTS, Q).astype(jnp.bfloat16)
    ramp_table = ramp_matrix(PTS)
    filtered = jnp.einsum("rtq,tu->rqu", patterns.astype(jnp.float32), ramp_table.astype(jnp.float32)).astype(jnp.bfloat16)
    thetas = angle_index.astype(jnp.float32) * (math.pi / NANG)
    row_coord = jnp.arange(ROWS).astype(jnp.float32) - (ROWS - 1) / 2.0
    col_coord = jnp.arange(COLS).astype(jnp.float32) - (COLS - 1) / 2.0
    center = (PTS - 1) / 2.0

    def one_rotation(running, element):
        sinogram, theta_now = element
        position = col_coord[None, :] * jnp.cos(theta_now) + row_coord[:, None] * jnp.sin(theta_now) + center
        floor_pos = jnp.floor(position)
        for step_ahead in (0.0, 1.0):
            tap_point = floor_pos + step_ahead
            rounded = lax.optimization_barrier(jnp.maximum(0.0, 1.0 - jnp.abs(tap_point - position)).astype(jnp.bfloat16))
            weight = rounded.astype(jnp.float32)
            inside = (tap_point >= 0.0) & (tap_point <= PTS - 1.0)
            tap_index = jnp.clip(tap_point, 0.0, PTS - 1.0).astype(jnp.int32)
            values_here = jnp.take(sinogram, tap_index, axis=1).astype(jnp.float32)
            running = running + values_here * jnp.where(inside, weight, 0.0)[None]
        return running, None

    def one_group(sinograms):
        empty_slab = jnp.zeros((sinograms.shape[1], ROWS, COLS), jnp.float32)
        result, unused = lax.scan(one_rotation, empty_slab, (sinograms, thetas))
        return result.astype(jnp.bfloat16)

    grouped = filtered.reshape(ROT, QBLK, TILE, PTS).transpose(1, 0, 2, 3)
    return lax.map(one_group, grouped).reshape(Q, ROWS, COLS)
```

```python
import functools
import math

import jax
import jax.numpy as jnp
from jax import lax
from jax.experimental import pallas as pl
from jax.experimental.pallas import tpu as pltpu
from jax.sharding import PartitionSpec as P

NANG = 180
ROWS_DEV = 8
COLS = 2048
LANES = 128
VMEM_LIMIT = 60 * 2**20


def ramp_rows(t_index, points):
    offset = t_index[:, None] - jnp.arange(points)[None, :]
    is_odd = offset % 2 == 1
    distance = offset.astype(jnp.float32)
    safe_offset = jnp.where(is_odd, distance, 1.0)
    kernel = jnp.where(is_odd, -1.0 / (math.pi * math.pi * safe_offset * safe_offset), 0.0)
    kernel = jnp.where(offset == 0, 0.25, kernel)
    return kernel.astype(jnp.bfloat16)


def integrate_kernel(blocks, index_ref, mask_ref, pix_ref, frames_ref, values_ref, mine_ref, other_ref):
    step = pl.program_id(0)
    p = pix_ref[0]
    entries, tile_size = values_ref.shape[1], values_ref.shape[2]
    tiles_dev = frames_ref.shape[2] // tile_size
    for j in range(blocks):
        block = step * blocks + j
        halves = []
        for half in (p, 1 - p):
            pieces = []
            for k in range(entries):
                tile = index_ref[block, k] - p * tiles_dev
                where = pl.ds(pl.multiple_of(tile * tile_size, tile_size), tile_size)
                pieces.append(frames_ref[half, :, where] * mask_ref[block, k].astype(jnp.bfloat16))
            halves.append(jnp.concatenate(pieces, axis=1))
        rows = halves[0].shape[0]
        sums = jnp.dot(
            jnp.concatenate(halves, axis=0),
            values_ref[j].reshape(entries * tile_size, tile_size),
            preferred_element_type=jnp.float32,
        )
        for ref, part in ((mine_ref, sums[:rows]), (other_ref, sums[rows:])):
            width = ref.shape[2]
            if width >= tile_size:
                ref[0, :, j * tile_size : (j + 1) * tile_size] = part.astype(ref.dtype)
            else:
                for i in range(tile_size // width):
                    ref[i] = part[:, i * width : (i + 1) * width].astype(ref.dtype)


def integrate(frames, tile_values, tile_index, tile_mask, scan_count):
    rot_dev, pts_dev, row_width = frames.shape
    qblocks, entries, tile_size, _ = tile_values.shape
    q_local = qblocks * tile_size // scan_count
    rows = rot_dev * pts_dev // 2
    blocks = max(1, q_local // tile_size)
    owners = max(1, tile_size // q_local)
    part_spec = pl.BlockSpec((owners, rows, q_local), lambda i: (i, 0, 0))
    return pl.pallas_call(
        functools.partial(integrate_kernel, blocks),
        grid=(qblocks // blocks,),
        in_specs=[
            pl.BlockSpec(memory_space=pltpu.SMEM),
            pl.BlockSpec(memory_space=pltpu.SMEM),
            pl.BlockSpec(memory_space=pltpu.SMEM),
            pl.BlockSpec((2, rows, row_width), lambda i: (0, 0, 0)),
            pl.BlockSpec((blocks, entries, tile_size, tile_size), lambda i: (i, 0, 0, 0)),
        ],
        out_specs=[part_spec, part_spec],
        out_shape=[
            jax.ShapeDtypeStruct((scan_count, rows, q_local), jnp.float32),
            jax.ShapeDtypeStruct((scan_count, rows, q_local), jnp.bfloat16),
        ],
        compiler_params=pltpu.CompilerParams(vmem_limit_bytes=VMEM_LIMIT),
        name="integrate",
    )(
        tile_index,
        tile_mask,
        lax.axis_index("pix").astype(jnp.int32).reshape(1),
        frames.reshape(2, rows, row_width),
        tile_values,
    )


def backproject_kernel(groups, *refs):
    cos_ref, sin_ref, row_ref = refs[:3]
    pattern_refs = refs[3 : 3 + groups]
    ramp_ref, out_ref, filtered_ref, weight_ref, turned_ref, list_ref = refs[3 + groups :]
    parts, rot_group, pts, q_local = pattern_refs[0].shape
    points = parts * pts
    rotations = groups * rot_group
    segments = points // LANES
    slots = rotations * segments
    column_block = pl.program_id(0)

    @pl.when(column_block == 0)
    def _():
        for g in range(groups):
            for i in range(rot_group):
                patterns = pattern_refs[g][:, i].reshape(points, q_local)
                filtered = lax.dot_general(
                    patterns,
                    ramp_ref[...],
                    (((0,), (0,)), ((), ())),
                    preferred_element_type=jnp.float32,
                )
                at = (g * rot_group + i) * points
                filtered_ref[:, at : at + points] = filtered.astype(jnp.bfloat16)

    center = (points - 1) / 2.0
    x_first = (column_block * LANES).astype(jnp.float32) - (COLS - 1) / 2.0
    x_last = x_first + (LANES - 1.0)
    y_first = row_ref[0]
    y_last = y_first + (ROWS_DEV - 1.0)
    count = jnp.int32(0)
    spare = jnp.int32(0)
    for r in range(rotations):
        x_a, x_b = x_first * cos_ref[r], x_last * cos_ref[r]
        y_a, y_b = y_first * sin_ref[r], y_last * sin_ref[r]
        low = jnp.minimum(x_a, x_b) + jnp.minimum(y_a, y_b) + center
        high = jnp.maximum(x_a, x_b) + jnp.maximum(y_a, y_b) + center
        for segment in range(segments):
            first = segment * LANES
            active = jnp.logical_and(high > first - 1.5, low < first + LANES + 0.5)
            slot = r * segments + segment
            list_ref[count] = jnp.int32(slot)
            spare = jnp.where(active, spare, slot)
            count = jnp.where(active, count + 1, count)
    list_ref[count] = spare

    x = x_first + lax.broadcasted_iota(jnp.int32, (ROWS_DEV, LANES), 1).astype(jnp.float32)
    y = y_first + lax.broadcasted_iota(jnp.int32, (ROWS_DEV, LANES), 0).astype(jnp.float32)
    tap = lax.broadcasted_iota(jnp.int32, (LANES, LANES), 0).astype(jnp.float32)

    def put_weights(a):
        slot = list_ref[a]
        r = slot // segments
        position = x * cos_ref[r] + y * sin_ref[r] + center
        taps = tap + ((slot - r * segments) * LANES).astype(jnp.float32) if segments > 1 else tap
        for row in range(ROWS_DEV):
            weight = jnp.maximum(0.0, 1.0 - jnp.abs(taps - position[row : row + 1, :]))
            weight_ref[a * LANES : (a + 1) * LANES, row * LANES : (row + 1) * LANES] = weight.astype(
                jnp.bfloat16
            )

    pairs = (count + 1) // 2
    for m in range(1, rotations * min(segments, 3) // 2 + 1):

        @pl.when(pairs == m)
        def _(m=m):
            for a in range(2 * m):
                put_weights(a)
            taken = jnp.concatenate(
                [
                    filtered_ref[:, pl.ds(pl.multiple_of(list_ref[a] * LANES, LANES), LANES)]
                    for a in range(2 * m)
                ],
                axis=1,
            )
            for row in range(0, ROWS_DEV, 2):
                sums = jnp.dot(
                    taken,
                    weight_ref[: 2 * m * LANES, row * LANES : (row + 2) * LANES],
                    preferred_element_type=jnp.float32,
                )
                for i in range(2):
                    turned_ref[pl.ds(row + i, q_local, stride=ROWS_DEV), :] = sums[
                        :, i * LANES : (i + 1) * LANES
                    ]
            out_ref[...] = turned_ref[...].reshape(q_local, ROWS_DEV, LANES).astype(jnp.bfloat16)

    @pl.when(pairs == 0)
    def _():
        out_ref[...] = jnp.zeros(out_ref.shape, jnp.bfloat16)


def backproject(cosines, sines, row_first, patterns, ramp_table):
    groups = len(patterns)
    parts, rot_group, pts, q_local = patterns[0].shape
    points = parts * pts
    slots = groups * rot_group * points // LANES
    return pl.pallas_call(
        functools.partial(backproject_kernel, groups),
        grid=(COLS // LANES,),
        in_specs=[pl.BlockSpec(memory_space=pltpu.SMEM)] * 3
        + [pl.BlockSpec(patterns[0].shape, lambda i: (0, 0, 0, 0))] * groups
        + [pl.BlockSpec((points, points), lambda i: (0, 0))],
        out_specs=pl.BlockSpec((q_local, ROWS_DEV, LANES), lambda i: (0, 0, i)),
        out_shape=jax.ShapeDtypeStruct((q_local, ROWS_DEV, COLS), jnp.bfloat16),
        scratch_shapes=[
            pltpu.VMEM((q_local, groups * rot_group * points), jnp.bfloat16),
            pltpu.VMEM((slots * LANES, ROWS_DEV * LANES), jnp.bfloat16),
            pltpu.VMEM((q_local * ROWS_DEV, LANES), jnp.float32),
            pltpu.SMEM((slots + 1,), jnp.int32),
        ],
        compiler_params=pltpu.CompilerParams(vmem_limit_bytes=VMEM_LIMIT),
        name="backproject",
    )(cosines, sines, row_first, *patterns, ramp_table)


def shift(x, axis, by):
    size = lax.axis_size(axis)
    return lax.ppermute(x, axis, [(i, (i + by) % size) for i in range(size)])


def shards(frames, tile_values, tile_index, tile_mask, angle_index):
    rot_dev, pts_dev, row_width = frames.shape
    scan_count = lax.axis_size("scan")
    view_count = lax.axis_size("view")
    points = pts_dev * scan_count
    s, v, p = lax.axis_index("scan"), lax.axis_index("view"), lax.axis_index("pix")
    rot_half = rot_dev // 2

    mine, other = integrate(frames, tile_values, tile_index, tile_mask, scan_count)
    q_local = mine.shape[2]
    patterns = (mine + shift(other, "pix", 1).astype(jnp.float32)).astype(jnp.bfloat16)

    if scan_count <= 4:
        pieces = [
            shift(lax.dynamic_index_in_dim(patterns, (s + d) % scan_count, 0), "scan", d)
            for d in range(1, scan_count)
        ]
        own = lax.dynamic_index_in_dim(patterns, s, 0)
        gathered = jnp.concatenate([own] + pieces, axis=0)
        source = (s - jnp.arange(scan_count)) % scan_count
    else:
        gathered = lax.all_to_all(patterns, "scan", split_axis=0, concat_axis=0, tiled=True)
        source = jnp.arange(scan_count)
    gathered = gathered.reshape(scan_count, rot_half, pts_dev, q_local)

    arrays, first_rotation = [], []
    for d in range(view_count):
        here = shift(gathered, "view", d) if d else gathered
        start = ((v - d) % view_count) * rot_dev
        arrays += [here, shift(here, "pix", 1)]
        first_rotation += [start + p * rot_half, start + (1 - p) * rot_half]

    order = (jnp.stack(first_rotation)[:, None] + jnp.arange(rot_half)[None, :]).reshape(-1)
    thetas = angle_index.astype(jnp.float32) * (math.pi / NANG)
    cosines = jnp.take(jnp.cos(thetas), order)
    sines = jnp.take(jnp.sin(thetas), order)
    rows_all = ROWS_DEV * view_count * lax.axis_size("pix")
    row_first = ((v * lax.axis_size("pix") + p) * ROWS_DEV).astype(jnp.float32) - (rows_all - 1) / 2.0
    t_index = (source[:, None] * pts_dev + jnp.arange(pts_dev)[None, :]).reshape(-1)
    return backproject(
        cosines, sines, row_first.reshape(1), arrays, ramp_rows(t_index, points)
    )


def solution(mesh):
    return jax.shard_map(
        shards,
        mesh=mesh,
        in_specs=(
            P(("grp", "view"), "scan", "pix"),
            P(None, "pix", None, None),
            P(None, "pix"),
            P(None, "pix"),
            P(),
        ),
        out_specs=P(("grp", "scan"), ("view", "pix"), None),
        check_vma=False,
    )
```

```python
import functools
import math

import jax
import jax.numpy as jnp
from jax import lax
from jax.experimental import pallas as pl
from jax.experimental.pallas import tpu as pltpu
from jax.sharding import PartitionSpec as P

NANG = 180
ROWS_DEV = 8
COLS = 2048
LANES = 128
VMEM_LIMIT = 60 * 2**20


def ramp_rows(t_index, points):
    offset = t_index[:, None] - jnp.arange(points)[None, :]
    is_odd = offset % 2 == 1
    distance = offset.astype(jnp.float32)
    safe_offset = jnp.where(is_odd, distance, 1.0)
    kernel = jnp.where(is_odd, -1.0 / (math.pi * math.pi * safe_offset * safe_offset), 0.0)
    kernel = jnp.where(offset == 0, 0.25, kernel)
    return kernel.astype(jnp.bfloat16)


def integrate_kernel(blocks, index_ref, mask_ref, pix_ref, frames_ref, values_ref, mine_ref, other_ref):
    step = pl.program_id(0)
    p = pix_ref[0]
    entries, tile_size = values_ref.shape[1], values_ref.shape[2]
    tiles_dev = frames_ref.shape[2] // tile_size
    for j in range(blocks):
        block = step * blocks + j
        halves = []
        for half in (p, 1 - p):
            pieces = []
            for k in range(entries):
                tile = index_ref[k, block] - p * tiles_dev
                where = pl.ds(pl.multiple_of(tile * tile_size, tile_size), tile_size)
                pieces.append(frames_ref[half, :, where] * mask_ref[k, block].astype(jnp.bfloat16))
            halves.append(jnp.concatenate(pieces, axis=1))
        rows = halves[0].shape[0]
        sums = jnp.dot(
            jnp.concatenate(halves, axis=0),
            values_ref[j].reshape(entries * tile_size, tile_size),
            preferred_element_type=jnp.float32,
        )
        for ref, part in ((mine_ref, sums[:rows]), (other_ref, sums[rows:])):
            width = ref.shape[2]
            if width >= tile_size:
                owner, at = divmod(j * tile_size, width)
                ref[owner, :, at : at + tile_size] = part.astype(ref.dtype)
            else:
                each = tile_size // width
                for i in range(each):
                    ref[j * each + i] = part[:, i * width : (i + 1) * width].astype(ref.dtype)


def integrate(frames, tile_values, tile_index, tile_mask, scan_count):
    rot_dev, pts_dev, row_width = frames.shape
    qblocks, entries, tile_size, _ = tile_values.shape
    q_local = qblocks * tile_size // scan_count
    rows = rot_dev * pts_dev // 2
    steps = 2
    blocks = qblocks // steps
    owners = scan_count // steps
    part_spec = pl.BlockSpec((owners, rows, q_local), lambda i: (i, 0, 0))
    return pl.pallas_call(
        functools.partial(integrate_kernel, blocks),
        grid=(steps,),
        in_specs=[
            pl.BlockSpec(memory_space=pltpu.SMEM),
            pl.BlockSpec(memory_space=pltpu.SMEM),
            pl.BlockSpec(memory_space=pltpu.SMEM),
            pl.BlockSpec((2, rows, row_width), lambda i: (0, 0, 0)),
            pl.BlockSpec((blocks, entries, tile_size, tile_size), lambda i: (i, 0, 0, 0)),
        ],
        out_specs=[part_spec, part_spec],
        out_shape=[
            jax.ShapeDtypeStruct((scan_count, rows, q_local), jnp.float32),
            jax.ShapeDtypeStruct((scan_count, rows, q_local), jnp.bfloat16),
        ],
        compiler_params=pltpu.CompilerParams(vmem_limit_bytes=VMEM_LIMIT),
        name="integrate",
    )(
        tile_index.T,
        tile_mask.T,
        lax.axis_index("pix").astype(jnp.int32).reshape(1),
        frames.reshape(2, rows, row_width),
        tile_values,
    )


UNIT = 2 * LANES


def active_lists(cosines, sines, row_first, points):
    segments = points // LANES
    center = (points - 1) / 2.0
    x_first = (jnp.arange(COLS // LANES) * LANES).astype(jnp.float32)[:, None] - (COLS - 1) / 2.0
    x_a, x_b = x_first * cosines, (x_first + (LANES - 1.0)) * cosines
    y_a, y_b = row_first * sines, (row_first + (ROWS_DEV - 1.0)) * sines
    low = jnp.minimum(x_a, x_b) + jnp.minimum(y_a, y_b) + center
    high = jnp.maximum(x_a, x_b) + jnp.maximum(y_a, y_b) + center
    first = (jnp.arange(segments) * LANES).astype(jnp.float32)
    active = (high[:, :, None] > first - 1.5) & (low[:, :, None] < first + (LANES + 0.5))
    active = active.reshape(COLS // LANES, -1)
    slots = active.shape[1]
    number = jnp.arange(slots)
    key = jnp.where(active, 0, slots) + number
    rank = jnp.sum((key[:, :, None] > key[:, None, :]).astype(jnp.int32), axis=2)
    lists = jnp.sum(jnp.where(rank[:, :, None] == number, number[None, :, None], 0), axis=1)
    counts = jnp.sum(active.astype(jnp.int32), axis=1)
    unit_counts = jnp.max(counts.reshape(COLS // UNIT, UNIT // LANES), axis=1)
    half = COLS // UNIT // 2
    pairs = (jnp.maximum(unit_counts[:half][::-1], unit_counts[half:]) + 1) // 2
    return pairs, lists


def backproject_kernel(group_sizes, *refs):
    pairs_ref, lists_ref, cos_ref, sin_ref, row_ref = refs[:5]
    total = sum(group_sizes)
    pattern_refs = refs[5 : 5 + total]
    ramp_ref, out_ref, filtered_ref, stage_ref, sems = refs[5 + total : 10 + total]
    turned_refs = refs[10 + total :]
    _, rot_group, pts, q_local = pattern_refs[0].shape
    points = ramp_ref.shape[0]
    segments = points // LANES
    rotations = len(group_sizes) * rot_group
    group, groups = pl.program_id(0), pl.num_programs(0)

    @pl.when(group == 0)
    def _():
        at = 0
        number = 0
        for size in group_sizes:
            for i in range(rot_group):
                patterns = jnp.concatenate(
                    [ref[:, i].reshape(-1, q_local) for ref in pattern_refs[number : number + size]], axis=0
                )
                filtered = lax.dot_general(
                    patterns,
                    ramp_ref[...],
                    (((0,), (0,)), ((), ())),
                    preferred_element_type=jnp.float32,
                )
                filtered_ref[:, at : at + points] = filtered.astype(jnp.bfloat16)
                at += points
            number += size

    center = (points - 1) / 2.0
    y_first = row_ref[0]
    buffer = lax.rem(group, 2)
    units = (groups - 1 - group, groups + group)

    def copy_out(side, which):
        columns = pl.ds(pl.multiple_of(units[side] * UNIT, UNIT), UNIT)
        return pltpu.make_async_copy(stage_ref.at[which, side], out_ref.at[:, :, columns], sems.at[which, side])

    @pl.when(group >= 2)
    def _():
        for side in range(2):
            copy_out(side, buffer).wait()

    pairs = pairs_ref[group]
    most = rotations * min(segments, 3) // 2
    sizes = [n for n in (1, 2, 4, 8) if n < most] + [most]
    for fewer, m in zip([0] + sizes, sizes):

        @pl.when(jnp.logical_and(pairs > fewer, pairs <= m))
        def _(m=m):
            tap = lax.broadcasted_iota(jnp.int32, (LANES, LANES), 0).astype(jnp.float32)

            def cast(side, rows):
                both = [
                    ref[rows.start * ROWS_DEV : rows.stop * ROWS_DEV, :]
                    for ref in turned_refs[2 * side : 2 * side + 2]
                ]
                stage_ref[buffer, side, rows] = (
                    jnp.concatenate(both, axis=1)
                    .reshape(rows.stop - rows.start, ROWS_DEV, UNIT)
                    .astype(jnp.bfloat16)
                )

            for k in range(4):
                block = units[k // 2] * 2 + k % 2
                x_first = (block * LANES).astype(jnp.float32) - (COLS - 1) / 2.0
                x = x_first + lax.broadcasted_iota(jnp.int32, (ROWS_DEV, LANES), 1).astype(jnp.float32)
                y = y_first + lax.broadcasted_iota(jnp.int32, (ROWS_DEV, LANES), 0).astype(jnp.float32)
                slots = [lists_ref[block, a] for a in range(2 * m)]
                positions = []
                for slot in slots:
                    r = slot // segments
                    position = x * cos_ref[r] + y * sin_ref[r] + center
                    if segments > 1:
                        position = position - ((slot - r * segments) * LANES).astype(jnp.float32)
                    positions.append(position)
                taken = jnp.concatenate(
                    [filtered_ref[:, pl.ds(pl.multiple_of(slot * LANES, LANES), LANES)] for slot in slots],
                    axis=1,
                )

                def weights(position, row):
                    return jnp.maximum(0.0, 1.0 - jnp.abs(tap - position[row : row + 1, :])).astype(
                        jnp.bfloat16
                    )

                for row in range(0, ROWS_DEV, 2):
                    two_rows = jnp.concatenate(
                        [
                            jnp.concatenate([weights(position, row + i) for i in range(2)], axis=1)
                            for position in positions
                        ],
                        axis=0,
                    )
                    sums = jnp.dot(taken, two_rows, preferred_element_type=jnp.float32)
                    for i in range(2):
                        turned_refs[k][pl.ds(row + i, q_local, stride=ROWS_DEV), :] = sums[
                            :, i * LANES : (i + 1) * LANES
                        ]
                    if k >= 2:
                        part = q_local // 8
                        at = ((k - 2) * 4 + row // 2) * part
                        cast(0, slice(at, at + part))
            cast(1, slice(0, q_local))

    @pl.when(pairs == 0)
    def _():
        stage_ref[buffer] = jnp.zeros(stage_ref.shape[1:], jnp.bfloat16)

    for side in range(2):
        copy_out(side, buffer).start()

    @pl.when(group == groups - 1)
    def _():
        for which in (1 - buffer, buffer):
            for side in range(2):
                copy_out(side, which).wait()


def backproject(cosines, sines, row_first, patterns, ramp_table):
    group_sizes = tuple(len(group) for group in patterns)
    arrays = [array for group in patterns for array in group]
    _, rot_group, pts, q_local = arrays[0].shape
    points = ramp_table.shape[0]
    pairs, lists = active_lists(cosines, sines, row_first, points)
    return pl.pallas_call(
        functools.partial(backproject_kernel, group_sizes),
        grid=(COLS // (2 * UNIT),),
        in_specs=[pl.BlockSpec(memory_space=pltpu.SMEM)] * 5
        + [pl.BlockSpec(array.shape, lambda i: (0, 0, 0, 0)) for array in arrays]
        + [pl.BlockSpec((points, points), lambda i: (0, 0))],
        out_specs=pl.BlockSpec(memory_space=pl.ANY),
        out_shape=jax.ShapeDtypeStruct((q_local, ROWS_DEV, COLS), jnp.bfloat16),
        scratch_shapes=[
            pltpu.VMEM((q_local, len(patterns) * rot_group * points), jnp.bfloat16),
            pltpu.VMEM((2, 2, q_local, ROWS_DEV, UNIT), jnp.bfloat16),
            pltpu.SemaphoreType.DMA((2, 2)),
        ]
        + [pltpu.VMEM((q_local * ROWS_DEV, LANES), jnp.float32)] * 4,
        compiler_params=pltpu.CompilerParams(vmem_limit_bytes=VMEM_LIMIT),
        name="backproject",
    )(pairs, lists, cosines, sines, row_first.reshape(1), *arrays, ramp_table)


def shift(x, axis, by):
    size = lax.axis_size(axis)
    return lax.ppermute(x, axis, [(i, (i + by) % size) for i in range(size)])


def shards(frames, tile_values, tile_index, tile_mask, angle_index):
    rot_dev, pts_dev, row_width = frames.shape
    scan_count = lax.axis_size("scan")
    view_count = lax.axis_size("view")
    points = pts_dev * scan_count
    s, v, p = lax.axis_index("scan"), lax.axis_index("view"), lax.axis_index("pix")
    rot_half = rot_dev // 2

    mine, other = integrate(frames, tile_values, tile_index, tile_mask, scan_count)
    q_local = mine.shape[2]
    patterns = (mine + shift(other, "pix", 1).astype(jnp.float32)).astype(jnp.bfloat16)

    def per_rotation(x):
        return x.reshape(-1, rot_half, pts_dev, q_local)

    if scan_count == 4 and view_count == 2:
        own, to_1, to_2, to_3 = [lax.dynamic_index_in_dim(patterns, (s + d) % 4, 0) for d in range(4)]
        from_2, from_1, from_3 = shift(to_2, "scan", 2), shift(to_1, "scan", 1), shift(to_3, "scan", 3)
        near = jnp.concatenate([from_1, from_3], axis=0)
        here = [own, near, from_2]
        there = [shift(x, "view", 1) for x in here]
        here_other = [shift(jnp.concatenate(here, axis=0), "pix", 1)]
        there_other = [shift(jnp.concatenate(there[:2], axis=0), "pix", 1), shift(there[2], "pix", 1)]
        arrays = [here, here_other, there, there_other]
        source = (s - jnp.array([0, 1, 3, 2])) % 4
    else:
        gathered = lax.all_to_all(patterns, "scan", split_axis=0, concat_axis=0, tiled=True)
        source = jnp.arange(scan_count)
        arrays = []
        for d in range(view_count):
            here = shift(gathered, "view", d) if d else gathered
            arrays += [[here], [shift(here, "pix", 1)]]
    arrays = [[per_rotation(x) for x in group] for group in arrays]

    first_rotation = []
    for d in range(view_count):
        start = ((v - d) % view_count) * rot_dev
        first_rotation += [start + p * rot_half, start + (1 - p) * rot_half]
    order = (jnp.stack(first_rotation)[:, None] + jnp.arange(rot_half)[None, :]).reshape(-1)
    thetas = angle_index.astype(jnp.float32) * (math.pi / NANG)
    cosines = jnp.take(jnp.cos(thetas), order)
    sines = jnp.take(jnp.sin(thetas), order)
    rows_all = ROWS_DEV * view_count * lax.axis_size("pix")
    row_first = ((v * lax.axis_size("pix") + p) * ROWS_DEV).astype(jnp.float32) - (rows_all - 1) / 2.0
    t_index = (source[:, None] * pts_dev + jnp.arange(pts_dev)[None, :]).reshape(-1)
    return backproject(cosines, sines, row_first, arrays, ramp_rows(t_index, points))


def solution(mesh):
    return jax.shard_map(
        shards,
        mesh=mesh,
        in_specs=(
            P(("grp", "view"), "scan", "pix"),
            P(None, "pix", None, None),
            P(None, "pix"),
            P(None, "pix"),
            P(),
        ),
        out_specs=P(("grp", "scan"), ("view", "pix"), None),
        check_vma=False,
    )
```

```python
import functools
import math

import jax
import jax.numpy as jnp
from jax import lax
from jax.experimental import pallas as pl
from jax.experimental.pallas import tpu as pltpu
from jax.sharding import PartitionSpec as P

NANG = 180
ROWS_DEV = 8
COLS = 2048
LANES = 128
VMEM_LIMIT = 60 * 2**20


def ramp_rows(t_index, points):
    offset = t_index[:, None] - jnp.arange(points)[None, :]
    is_odd = offset % 2 == 1
    distance = offset.astype(jnp.float32)
    safe_offset = jnp.where(is_odd, distance, 1.0)
    kernel = jnp.where(is_odd, -1.0 / (math.pi * math.pi * safe_offset * safe_offset), 0.0)
    kernel = jnp.where(offset == 0, 0.25, kernel)
    return kernel.astype(jnp.bfloat16)


def integrate_kernel(blocks, index_ref, mask_ref, pix_ref, frames_ref, values_ref, mine_ref, other_ref):
    step = pl.program_id(0)
    p = pix_ref[0]
    entries, tile_size = values_ref.shape[1], values_ref.shape[2]
    tiles_dev = frames_ref.shape[2] // tile_size
    for j in range(blocks):
        block = step * blocks + j
        halves = []
        for half in (p, 1 - p):
            pieces = []
            for k in range(entries):
                tile = index_ref[k, block] - p * tiles_dev
                where = pl.ds(pl.multiple_of(tile * tile_size, tile_size), tile_size)
                pieces.append(frames_ref[half, :, where] * mask_ref[k, block].astype(jnp.bfloat16))
            halves.append(jnp.concatenate(pieces, axis=1))
        rows = halves[0].shape[0]
        sums = jnp.dot(
            jnp.concatenate(halves, axis=0),
            values_ref[j].reshape(entries * tile_size, tile_size),
            preferred_element_type=jnp.float32,
        )
        for ref, part in ((mine_ref, sums[:rows]), (other_ref, sums[rows:])):
            width = ref.shape[2]
            if width >= tile_size:
                owner, at = divmod(j * tile_size, width)
                ref[owner, :, at : at + tile_size] = part.astype(ref.dtype)
            else:
                each = tile_size // width
                for i in range(each):
                    ref[j * each + i] = part[:, i * width : (i + 1) * width].astype(ref.dtype)


def integrate(frames, tile_values, tile_index, tile_mask, scan_count):
    rot_dev, pts_dev, row_width = frames.shape
    qblocks, entries, tile_size, _ = tile_values.shape
    q_local = qblocks * tile_size // scan_count
    rows = rot_dev * pts_dev // 2
    steps = 2
    blocks = qblocks // steps
    owners = scan_count // steps
    part_spec = pl.BlockSpec((owners, rows, q_local), lambda i: (i, 0, 0))
    return pl.pallas_call(
        functools.partial(integrate_kernel, blocks),
        grid=(steps,),
        in_specs=[
            pl.BlockSpec(memory_space=pltpu.SMEM),
            pl.BlockSpec(memory_space=pltpu.SMEM),
            pl.BlockSpec(memory_space=pltpu.SMEM),
            pl.BlockSpec((2, rows, row_width), lambda i: (0, 0, 0)),
            pl.BlockSpec((blocks, entries, tile_size, tile_size), lambda i: (i, 0, 0, 0)),
        ],
        out_specs=[part_spec, part_spec],
        out_shape=[
            jax.ShapeDtypeStruct((scan_count, rows, q_local), jnp.float32),
            jax.ShapeDtypeStruct((scan_count, rows, q_local), jnp.bfloat16),
        ],
        compiler_params=pltpu.CompilerParams(vmem_limit_bytes=VMEM_LIMIT),
        name="integrate",
    )(
        tile_index.T,
        tile_mask.T,
        lax.axis_index("pix").astype(jnp.int32).reshape(1),
        frames.reshape(2, rows, row_width),
        tile_values,
    )


UNIT = 2 * LANES


def active_lists(cosines, sines, row_first, points):
    segments = points // LANES
    center = (points - 1) / 2.0
    x_first = (jnp.arange(COLS // LANES) * LANES).astype(jnp.float32)[:, None] - (COLS - 1) / 2.0
    x_a, x_b = x_first * cosines, (x_first + (LANES - 1.0)) * cosines
    y_a, y_b = row_first * sines, (row_first + (ROWS_DEV - 1.0)) * sines
    low = jnp.minimum(x_a, x_b) + jnp.minimum(y_a, y_b) + center
    high = jnp.maximum(x_a, x_b) + jnp.maximum(y_a, y_b) + center
    first = (jnp.arange(segments) * LANES).astype(jnp.float32)
    active = (high[:, :, None] > first - 1.5) & (low[:, :, None] < first + (LANES + 0.5))
    active = active.reshape(COLS // LANES, -1)
    slots = active.shape[1]
    number = jnp.arange(slots)
    key = jnp.where(active, 0, slots) + number
    rank = jnp.sum((key[:, :, None] > key[:, None, :]).astype(jnp.int32), axis=2)
    lists = jnp.sum(jnp.where(rank[:, :, None] == number, number[None, :, None], 0), axis=1)
    counts = jnp.sum(active.astype(jnp.int32), axis=1)
    half = COLS // LANES // 2
    mirrored = jnp.maximum(counts[:half][::-1], counts[half:]).reshape(-1, 2)
    inner = jnp.max(mirrored, axis=1)
    pairs = (jnp.stack([inner, mirrored[:, 1]]) + 1) // 2
    return pairs, lists


def backproject_kernel(group_sizes, *refs):
    pairs_ref, lists_ref, cos_ref, sin_ref, row_ref = refs[:5]
    total = sum(group_sizes)
    pattern_refs = refs[5 : 5 + total]
    ramp_ref, out_ref, filtered_ref, stage_ref, sems = refs[5 + total : 10 + total]
    turned_refs = refs[10 + total :]
    _, rot_group, pts, q_local = pattern_refs[0].shape
    points = ramp_ref.shape[0]
    segments = points // LANES
    rotations = len(group_sizes) * rot_group
    group, groups = pl.program_id(0), pl.num_programs(0)

    @pl.when(group == 0)
    def _():
        at = 0
        number = 0
        for size in group_sizes:
            for i in range(rot_group):
                patterns = jnp.concatenate(
                    [ref[:, i].reshape(-1, q_local) for ref in pattern_refs[number : number + size]], axis=0
                )
                filtered = lax.dot_general(
                    patterns,
                    ramp_ref[...],
                    (((0,), (0,)), ((), ())),
                    preferred_element_type=jnp.float32,
                )
                filtered_ref[:, at : at + points] = filtered.astype(jnp.bfloat16)
                at += points
            number += size

    center = (points - 1) / 2.0
    y_first = row_ref[0]
    buffer = lax.rem(group, 2)
    units = (groups - 1 - group, groups + group)

    def copy_out(side, which, unit):
        columns = pl.ds(pl.multiple_of(unit * UNIT, UNIT), UNIT)
        return pltpu.make_async_copy(stage_ref.at[which, side], out_ref.at[:, :, columns], sems.at[which, side])

    @pl.when(group >= 2)
    def _():
        copy_out(0, buffer, units[0]).wait()

    @pl.when(group >= 3)
    def _():
        copy_out(1, 1 - buffer, units[1]).wait()

    def cast(side, which, start, stop):
        both = [ref[start * ROWS_DEV : stop * ROWS_DEV, :] for ref in turned_refs[2 * side : 2 * side + 2]]
        stage_ref[which, side, start:stop] = (
            jnp.concatenate(both, axis=1).reshape(stop - start, ROWS_DEV, UNIT).astype(jnp.bfloat16)
        )

    def send_previous():
        @pl.when(group >= 1)
        def _():
            copy_out(1, 1 - buffer, units[1] - 1).start()

    def multiply(m_inner, m_outer):
        tap = lax.broadcasted_iota(jnp.int32, (LANES, LANES), 0).astype(jnp.float32)

        def weights(position, row):
            return jnp.maximum(0.0, 1.0 - jnp.abs(tap - position[row : row + 1, :])).astype(jnp.bfloat16)

        for k in range(4):
            m = m_inner if k in (1, 2) else m_outer
            block = units[k // 2] * 2 + k % 2
            x_first = (block * LANES).astype(jnp.float32) - (COLS - 1) / 2.0
            x = x_first + lax.broadcasted_iota(jnp.int32, (ROWS_DEV, LANES), 1).astype(jnp.float32)
            y = y_first + lax.broadcasted_iota(jnp.int32, (ROWS_DEV, LANES), 0).astype(jnp.float32)
            slots = [lists_ref[block, a] for a in range(2 * m)]
            positions = []
            for slot in slots:
                r = slot // segments
                position = x * cos_ref[r] + y * sin_ref[r] + center
                if segments > 1:
                    position = position - ((slot - r * segments) * LANES).astype(jnp.float32)
                positions.append(position)
            taken = jnp.concatenate(
                [filtered_ref[:, pl.ds(pl.multiple_of(slot * LANES, LANES), LANES)] for slot in slots],
                axis=1,
            )
            for row in range(0, ROWS_DEV, 2):
                two_rows = jnp.concatenate(
                    [
                        jnp.concatenate([weights(position, row + i) for i in range(2)], axis=1)
                        for position in positions
                    ],
                    axis=0,
                )
                sums = jnp.dot(taken, two_rows, preferred_element_type=jnp.float32)
                part = q_local // 8
                at = ((k % 2) * 4 + row // 2) * part
                if k < 2:
                    cast(1, 1 - buffer, at, at + part)
                else:
                    cast(0, buffer, at, at + part)
                for i in range(2):
                    turned_refs[k][pl.ds(row + i, q_local, stride=ROWS_DEV), :] = sums[
                        :, i * LANES : (i + 1) * LANES
                    ]
            if k == 1:
                send_previous()

    inner, outer = pairs_ref[0, group], pairs_ref[1, group]
    most = rotations * min(segments, 3) // 2
    sizes = [n for n in (1, 2, 4, 8) if n < most] + [most]
    for fewer, m in zip([0] + sizes, sizes):
        here = jnp.logical_and(inner > fewer, inner <= m)
        if most > 4:
            pl.when(here)(functools.partial(multiply, m, m))
            continue
        for outer_fewer, outer_m in zip([-1] + sizes, [n for n in sizes if n <= m]):
            there = jnp.logical_and(outer > outer_fewer, outer <= outer_m)
            pl.when(jnp.logical_and(here, there))(functools.partial(multiply, m, outer_m))

    @pl.when(inner == 0)
    def _():
        cast(1, 1 - buffer, 0, q_local)
        send_previous()
        stage_ref[buffer, 0] = jnp.zeros(stage_ref.shape[2:], jnp.bfloat16)
        for ref in turned_refs[2:]:
            ref[...] = jnp.zeros(ref.shape, jnp.float32)

    copy_out(0, buffer, units[0]).start()

    @pl.when(group == groups - 1)
    def _():
        copy_out(1, buffer, units[1]).wait()
        cast(1, buffer, 0, q_local)
        copy_out(1, buffer, units[1]).start()
        for which in (1 - buffer, buffer):
            for side in range(2):
                copy_out(side, which, units[side]).wait()


def backproject(cosines, sines, row_first, patterns, ramp_table):
    group_sizes = tuple(len(group) for group in patterns)
    arrays = [array for group in patterns for array in group]
    _, rot_group, pts, q_local = arrays[0].shape
    points = ramp_table.shape[0]
    pairs, lists = active_lists(cosines, sines, row_first, points)
    return pl.pallas_call(
        functools.partial(backproject_kernel, group_sizes),
        grid=(COLS // (2 * UNIT),),
        in_specs=[pl.BlockSpec(memory_space=pltpu.SMEM)] * 5
        + [pl.BlockSpec(array.shape, lambda i: (0, 0, 0, 0)) for array in arrays]
        + [pl.BlockSpec((points, points), lambda i: (0, 0))],
        out_specs=pl.BlockSpec(memory_space=pl.ANY),
        out_shape=jax.ShapeDtypeStruct((q_local, ROWS_DEV, COLS), jnp.bfloat16),
        scratch_shapes=[
            pltpu.VMEM((q_local, len(patterns) * rot_group * points), jnp.bfloat16),
            pltpu.VMEM((2, 2, q_local, ROWS_DEV, UNIT), jnp.bfloat16),
            pltpu.SemaphoreType.DMA((2, 2)),
        ]
        + [pltpu.VMEM((q_local * ROWS_DEV, LANES), jnp.float32)] * 4,
        compiler_params=pltpu.CompilerParams(vmem_limit_bytes=VMEM_LIMIT),
        name="backproject",
    )(pairs, lists, cosines, sines, row_first.reshape(1), *arrays, ramp_table)


def shift(x, axis, by):
    size = lax.axis_size(axis)
    return lax.ppermute(x, axis, [(i, (i + by) % size) for i in range(size)])


def shards(frames, tile_values, tile_index, tile_mask, angle_index):
    rot_dev, pts_dev, row_width = frames.shape
    scan_count = lax.axis_size("scan")
    view_count = lax.axis_size("view")
    points = pts_dev * scan_count
    s, v, p = lax.axis_index("scan"), lax.axis_index("view"), lax.axis_index("pix")
    rot_half = rot_dev // 2

    mine, other = integrate(frames, tile_values, tile_index, tile_mask, scan_count)
    q_local = mine.shape[2]
    patterns = (mine + shift(other, "pix", 1).astype(jnp.float32)).astype(jnp.bfloat16)

    def per_rotation(x):
        return x.reshape(-1, rot_half, pts_dev, q_local)

    if scan_count == 4 and view_count == 2:
        own, to_1, to_2, to_3 = [lax.dynamic_index_in_dim(patterns, (s + d) % 4, 0) for d in range(4)]
        from_2, from_1, from_3 = shift(to_2, "scan", 2), shift(to_1, "scan", 1), shift(to_3, "scan", 3)
        near = jnp.concatenate([from_1, from_3], axis=0)
        here = [own, near, from_2]
        there = [shift(x, "view", 1) for x in here]
        here_other = [shift(jnp.concatenate(here, axis=0), "pix", 1)]
        there_other = [shift(jnp.concatenate(there[:2], axis=0), "pix", 1), shift(there[2], "pix", 1)]
        arrays = [here, here_other, there, there_other]
        steps = jnp.array([0, 1, 3, 2])
        own_patterns = own
    else:
        gathered = lax.all_to_all(patterns, "scan", split_axis=0, concat_axis=0, tiled=True)
        steps = None
        own_patterns = gathered
        arrays = []
        for d in range(view_count):
            here = shift(gathered, "view", d) if d else gathered
            arrays += [[here], [shift(here, "pix", 1)]]
    arrays = [[per_rotation(x) for x in group] for group in arrays]

    first_rotation = []
    for d in range(view_count):
        start = ((v - d) % view_count) * rot_dev
        first_rotation += [start + p * rot_half, start + (1 - p) * rot_half]
    order = (jnp.stack(first_rotation)[:, None] + jnp.arange(rot_half)[None, :]).reshape(-1)
    rotations = angle_index.shape[0]
    angles, s, v, p, _ = lax.optimization_barrier((angle_index, s, v, p, own_patterns))
    mine_first = jnp.sum(jnp.where(order[:, None] == jnp.arange(rotations), angles, 0), axis=1)
    thetas = mine_first.astype(jnp.float32) * (math.pi / NANG)
    cosines = jnp.cos(thetas)
    sines = jnp.sin(thetas)
    rows_all = ROWS_DEV * view_count * lax.axis_size("pix")
    row_first = ((v * lax.axis_size("pix") + p) * ROWS_DEV).astype(jnp.float32) - (rows_all - 1) / 2.0
    source = jnp.arange(scan_count) if steps is None else (s - steps) % scan_count
    t_index = (source[:, None] * pts_dev + jnp.arange(pts_dev)[None, :]).reshape(-1)
    return backproject(cosines, sines, row_first, arrays, ramp_rows(t_index, points))


def solution(mesh):
    return jax.shard_map(
        shards,
        mesh=mesh,
        in_specs=(
            P(("grp", "view"), "scan", "pix"),
            P(None, "pix", None, None),
            P(None, "pix"),
            P(None, "pix"),
            P(),
        ),
        out_specs=P(("grp", "scan"), ("view", "pix"), None),
        check_vma=False,
    )
```

```python
import functools
import math

import jax
import jax.numpy as jnp
from jax import lax
from jax.experimental import pallas as pl
from jax.experimental.pallas import tpu as pltpu
from jax.sharding import PartitionSpec as P

NANG = 180
ROWS_DEV = 8
COLS = 2048
LANES = 128
VMEM_LIMIT = 60 * 2**20


def ramp_rows(t_index, points):
    offset = t_index[:, None] - jnp.arange(points)[None, :]
    is_odd = offset % 2 == 1
    distance = offset.astype(jnp.float32)
    safe_offset = jnp.where(is_odd, distance, 1.0)
    kernel = jnp.where(is_odd, -1.0 / (math.pi * math.pi * safe_offset * safe_offset), 0.0)
    kernel = jnp.where(offset == 0, 0.25, kernel)
    return kernel.astype(jnp.bfloat16)


def integrate_kernel(blocks, index_ref, mask_ref, pix_ref, frames_ref, values_ref, mine_ref, other_ref):
    step = pl.program_id(0)
    p = pix_ref[0]
    entries, tile_size = values_ref.shape[1], values_ref.shape[2]
    tiles_dev = frames_ref.shape[2] // tile_size
    for j in range(blocks):
        block = step * blocks + j
        halves = []
        for half in (p, 1 - p):
            pieces = []
            for k in range(entries):
                tile = index_ref[k, block] - p * tiles_dev
                where = pl.ds(pl.multiple_of(tile * tile_size, tile_size), tile_size)
                pieces.append(frames_ref[half, :, where] * mask_ref[k, block].astype(jnp.bfloat16))
            halves.append(jnp.concatenate(pieces, axis=1))
        rows = halves[0].shape[0]
        sums = jnp.dot(
            jnp.concatenate(halves, axis=0),
            values_ref[j].reshape(entries * tile_size, tile_size),
            preferred_element_type=jnp.float32,
        )
        for ref, part in ((mine_ref, sums[:rows]), (other_ref, sums[rows:])):
            width = ref.shape[2]
            if width >= tile_size:
                owner, at = divmod(j * tile_size, width)
                ref[owner, :, at : at + tile_size] = part.astype(ref.dtype)
            else:
                each = tile_size // width
                for i in range(each):
                    ref[j * each + i] = part[:, i * width : (i + 1) * width].astype(ref.dtype)


def integrate(frames, tile_values, tile_index, tile_mask, scan_count):
    rot_dev, pts_dev, row_width = frames.shape
    qblocks, entries, tile_size, _ = tile_values.shape
    q_local = qblocks * tile_size // scan_count
    rows = rot_dev * pts_dev // 2
    steps = 2
    blocks = qblocks // steps
    owners = scan_count // steps
    part_spec = pl.BlockSpec((owners, rows, q_local), lambda i: (i, 0, 0))
    return pl.pallas_call(
        functools.partial(integrate_kernel, blocks),
        grid=(steps,),
        in_specs=[
            pl.BlockSpec(memory_space=pltpu.SMEM),
            pl.BlockSpec(memory_space=pltpu.SMEM),
            pl.BlockSpec(memory_space=pltpu.SMEM),
            pl.BlockSpec((2, rows, row_width), lambda i: (0, 0, 0)),
            pl.BlockSpec((blocks, entries, tile_size, tile_size), lambda i: (i, 0, 0, 0)),
        ],
        out_specs=[part_spec, part_spec],
        out_shape=[
            jax.ShapeDtypeStruct((scan_count, rows, q_local), jnp.bfloat16),
            jax.ShapeDtypeStruct((scan_count, rows, q_local), jnp.bfloat16),
        ],
        compiler_params=pltpu.CompilerParams(vmem_limit_bytes=VMEM_LIMIT),
        name="integrate",
    )(
        tile_index.T,
        tile_mask.T,
        lax.axis_index("pix").astype(jnp.int32).reshape(1),
        frames.reshape(2, rows, row_width),
        tile_values,
    )


UNIT = 2 * LANES


def active_lists(cosines, sines, row_first, points):
    segments = points // LANES
    center = (points - 1) / 2.0
    x_first = (jnp.arange(COLS // LANES) * LANES).astype(jnp.float32)[:, None] - (COLS - 1) / 2.0
    x_a, x_b = x_first * cosines, (x_first + (LANES - 1.0)) * cosines
    y_a, y_b = row_first * sines, (row_first + (ROWS_DEV - 1.0)) * sines
    low = jnp.minimum(x_a, x_b) + jnp.minimum(y_a, y_b) + center
    high = jnp.maximum(x_a, x_b) + jnp.maximum(y_a, y_b) + center
    first = (jnp.arange(segments) * LANES).astype(jnp.float32)
    active = (high[:, :, None] > first - 1.5) & (low[:, :, None] < first + (LANES + 0.5))
    active = active.reshape(COLS // LANES, -1)
    slots = active.shape[1]
    number = jnp.arange(slots)
    key = jnp.where(active, 0, slots) + number
    rank = jnp.sum((key[:, :, None] > key[:, None, :]).astype(jnp.int32), axis=2)
    lists = jnp.sum(jnp.where(rank[:, :, None] == number, number[None, :, None], 0), axis=1)
    counts = jnp.sum(active.astype(jnp.int32), axis=1)
    half = COLS // LANES // 2
    mirrored = jnp.maximum(counts[:half][::-1], counts[half:]).reshape(-1, 2)
    inner = jnp.max(mirrored, axis=1)
    pairs = (jnp.stack([inner, mirrored[:, 1]]) + 1) // 2
    return pairs, lists.T


def backproject_kernel(group_sizes, *refs):
    pairs_ref, lists_ref, cos_ref, sin_ref, row_ref = refs[:5]
    total = sum(group_sizes)
    pattern_refs = refs[5 : 5 + total]
    ramp_ref, out_ref, filtered_ref, stage_ref, sems = refs[5 + total : 10 + total]
    turned_refs = refs[10 + total :]
    _, rot_group, pts, q_local = pattern_refs[0].shape
    points = ramp_ref.shape[0]
    segments = points // LANES
    rotations = len(group_sizes) * rot_group
    group, groups = pl.program_id(0), pl.num_programs(0)

    @pl.when(group == 0)
    def _():
        at = 0
        number = 0
        for size in group_sizes:
            for i in range(rot_group):
                patterns = jnp.concatenate(
                    [ref[:, i].reshape(-1, q_local) for ref in pattern_refs[number : number + size]], axis=0
                )
                filtered = lax.dot_general(
                    patterns,
                    ramp_ref[...],
                    (((0,), (0,)), ((), ())),
                    preferred_element_type=jnp.float32,
                )
                filtered_ref[:, at : at + points] = filtered.astype(jnp.bfloat16)
                at += points
            number += size

    center = (points - 1) / 2.0
    y_first = row_ref[0]
    buffer = lax.rem(group, 2)
    units = (groups - 1 - group, groups + group)

    def copy_out(side, which, unit):
        columns = pl.ds(pl.multiple_of(unit * UNIT, UNIT), UNIT)
        return pltpu.make_async_copy(stage_ref.at[which, side], out_ref.at[:, :, columns], sems.at[which, side])

    @pl.when(group >= 2)
    def _():
        copy_out(0, buffer, units[0]).wait()

    @pl.when(group >= 3)
    def _():
        copy_out(1, 1 - buffer, units[1]).wait()

    def cast(side, which, start, stop):
        both = [ref[start * ROWS_DEV : stop * ROWS_DEV, :] for ref in turned_refs[2 * side : 2 * side + 2]]
        stage_ref[which, side, start:stop] = (
            jnp.concatenate(both, axis=1).reshape(stop - start, ROWS_DEV, UNIT).astype(jnp.bfloat16)
        )

    def send_previous():
        @pl.when(group >= 1)
        def _():
            copy_out(1, 1 - buffer, units[1] - 1).start()

    def multiply(m_inner, m_outer):
        tap = lax.broadcasted_iota(jnp.int32, (LANES, LANES), 0).astype(jnp.float32)

        def weights(position, row):
            return jnp.maximum(0.0, 1.0 - jnp.abs(tap - position[row : row + 1, :])).astype(jnp.bfloat16)

        for k in range(4):
            m = m_inner if k in (1, 2) else m_outer
            block = units[k // 2] * 2 + k % 2
            x_first = (block * LANES).astype(jnp.float32) - (COLS - 1) / 2.0
            x = x_first + lax.broadcasted_iota(jnp.int32, (ROWS_DEV, LANES), 1).astype(jnp.float32)
            y = y_first + lax.broadcasted_iota(jnp.int32, (ROWS_DEV, LANES), 0).astype(jnp.float32)
            slots = [lists_ref[a, block] for a in range(2 * m)]
            positions = []
            for slot in slots:
                r = slot // segments
                position = x * cos_ref[r] + y * sin_ref[r] + center
                if segments > 1:
                    position = position - ((slot - r * segments) * LANES).astype(jnp.float32)
                positions.append(position)
            taken = jnp.concatenate(
                [filtered_ref[:, pl.ds(pl.multiple_of(slot * LANES, LANES), LANES)] for slot in slots],
                axis=1,
            )
            for row in range(0, ROWS_DEV, 2):
                two_rows = jnp.concatenate(
                    [
                        jnp.concatenate([weights(position, row + i) for i in range(2)], axis=1)
                        for position in positions
                    ],
                    axis=0,
                )
                sums = jnp.dot(taken, two_rows, preferred_element_type=jnp.float32)
                part = q_local // 8
                at = ((k % 2) * 4 + row // 2) * part
                if k < 2:
                    cast(1, 1 - buffer, at, at + part)
                else:
                    cast(0, buffer, at, at + part)
                for i in range(2):
                    turned_refs[k][pl.ds(row + i, q_local, stride=ROWS_DEV), :] = sums[
                        :, i * LANES : (i + 1) * LANES
                    ]
            if k == 1:
                send_previous()

    inner, outer = pairs_ref[0, group], pairs_ref[1, group]
    most = rotations * min(segments, 3) // 2
    sizes = [n for n in (1, 2, 4, 8) if n < most] + [most]
    for fewer, m in zip([0] + sizes, sizes):
        here = jnp.logical_and(inner > fewer, inner <= m)
        if most > 4:
            pl.when(here)(functools.partial(multiply, m, m))
            continue
        for outer_fewer, outer_m in zip([-1] + sizes, [n for n in sizes if n <= m]):
            there = jnp.logical_and(outer > outer_fewer, outer <= outer_m)
            pl.when(jnp.logical_and(here, there))(functools.partial(multiply, m, outer_m))

    @pl.when(inner == 0)
    def _():
        cast(1, 1 - buffer, 0, q_local)
        send_previous()
        stage_ref[buffer, 0] = jnp.zeros(stage_ref.shape[2:], jnp.bfloat16)
        for ref in turned_refs[2:]:
            ref[...] = jnp.zeros(ref.shape, jnp.float32)

    copy_out(0, buffer, units[0]).start()

    @pl.when(group == groups - 1)
    def _():
        copy_out(1, buffer, units[1]).wait()
        cast(1, buffer, 0, q_local)
        copy_out(1, buffer, units[1]).start()
        for which in (1 - buffer, buffer):
            for side in range(2):
                copy_out(side, which, units[side]).wait()


def backproject(cosines, sines, row_first, patterns, ramp_table):
    group_sizes = tuple(len(group) for group in patterns)
    arrays = [array for group in patterns for array in group]
    _, rot_group, pts, q_local = arrays[0].shape
    points = ramp_table.shape[0]
    pairs, lists = active_lists(cosines, sines, row_first, points)
    return pl.pallas_call(
        functools.partial(backproject_kernel, group_sizes),
        grid=(COLS // (2 * UNIT),),
        in_specs=[pl.BlockSpec(memory_space=pltpu.SMEM)] * 5
        + [pl.BlockSpec(array.shape, lambda i: (0, 0, 0, 0)) for array in arrays]
        + [pl.BlockSpec((points, points), lambda i: (0, 0))],
        out_specs=pl.BlockSpec(memory_space=pl.ANY),
        out_shape=jax.ShapeDtypeStruct((q_local, ROWS_DEV, COLS), jnp.bfloat16),
        scratch_shapes=[
            pltpu.VMEM((q_local, len(patterns) * rot_group * points), jnp.bfloat16),
            pltpu.VMEM((2, 2, q_local, ROWS_DEV, UNIT), jnp.bfloat16),
            pltpu.SemaphoreType.DMA((2, 2)),
        ]
        + [pltpu.VMEM((q_local * ROWS_DEV, LANES), jnp.float32)] * 4,
        compiler_params=pltpu.CompilerParams(vmem_limit_bytes=VMEM_LIMIT),
        name="backproject",
    )(pairs, lists, cosines, sines, row_first.reshape(1), *arrays, ramp_table)


def shift(x, axis, by):
    size = lax.axis_size(axis)
    return lax.ppermute(x, axis, [(i, (i + by) % size) for i in range(size)])


def shards(frames, tile_values, tile_index, tile_mask, angle_index):
    rot_dev, pts_dev, row_width = frames.shape
    scan_count = lax.axis_size("scan")
    view_count = lax.axis_size("view")
    points = pts_dev * scan_count
    s, v, p = lax.axis_index("scan"), lax.axis_index("view"), lax.axis_index("pix")
    rot_half = rot_dev // 2

    mine, other = integrate(frames, tile_values, tile_index, tile_mask, scan_count)
    q_local = mine.shape[2]
    patterns = mine + shift(other, "pix", 1)

    def per_rotation(x):
        return x.reshape(-1, rot_half, pts_dev, q_local)

    if scan_count == 4 and view_count == 2:
        own, to_1, to_2, to_3 = [lax.dynamic_index_in_dim(patterns, (s + d) % 4, 0) for d in range(4)]
        from_2, from_1, from_3 = shift(to_2, "scan", 2), shift(to_1, "scan", 1), shift(to_3, "scan", 3)
        near = jnp.concatenate([from_1, from_3], axis=0)
        here = [own, near, from_2]
        there = [shift(x, "view", 1) for x in here]
        here_other = [shift(jnp.concatenate(here, axis=0), "pix", 1)]
        there_other = [shift(jnp.concatenate(there[:2], axis=0), "pix", 1), shift(there[2], "pix", 1)]
        arrays = [here, here_other, there, there_other]
        steps = jnp.array([0, 1, 3, 2])
        last_piece = from_2
    else:
        gathered = lax.all_to_all(patterns, "scan", split_axis=0, concat_axis=0, tiled=True)
        steps = None
        last_piece = gathered
        arrays = []
        for d in range(view_count):
            here = shift(gathered, "view", d) if d else gathered
            arrays += [[here], [shift(here, "pix", 1)]]
    arrays = [[per_rotation(x) for x in group] for group in arrays]

    first_rotation = []
    for d in range(view_count):
        start = ((v - d) % view_count) * rot_dev
        first_rotation += [start + p * rot_half, start + (1 - p) * rot_half]
    order = (jnp.stack(first_rotation)[:, None] + jnp.arange(rot_half)[None, :]).reshape(-1)
    rotations = angle_index.shape[0]
    angles, _ = lax.optimization_barrier((angle_index, last_piece))
    mine_first = jnp.sum(jnp.where(order[:, None] == jnp.arange(rotations), angles, 0), axis=1)
    thetas = mine_first.astype(jnp.float32) * (math.pi / NANG)
    cosines = jnp.cos(thetas)
    sines = jnp.sin(thetas)
    rows_all = ROWS_DEV * view_count * lax.axis_size("pix")
    row_first = ((v * lax.axis_size("pix") + p) * ROWS_DEV).astype(jnp.float32) - (rows_all - 1) / 2.0
    source = jnp.arange(scan_count) if steps is None else (s - steps) % scan_count
    t_index = (source[:, None] * pts_dev + jnp.arange(pts_dev)[None, :]).reshape(-1)
    return backproject(cosines, sines, row_first, arrays, ramp_rows(t_index, points))


def solution(mesh):
    return jax.shard_map(
        shards,
        mesh=mesh,
        in_specs=(
            P(("grp", "view"), "scan", "pix"),
            P(None, "pix", None, None),
            P(None, "pix"),
            P(None, "pix"),
            P(),
        ),
        out_specs=P(("grp", "scan"), ("view", "pix"), None),
        check_vma=False,
    )
```
